32 devices in a mesh: ctx: 8 (over z, x), exp: 4 (over y, core).
Axes of the slice: x: 2, y: 2, z: 4, core: 2. Of those that a mesh axis runs over, the one named last changes fastest.
Arguments:
- queries: bfloat16 [512, 6144], P('exp', 'ctx'), may hold values from -4 to 4
- key_vectors: bfloat16 [512, 6144], P('exp', 'ctx'), may hold values from -4 to 4
- value_vectors: bfloat16 [512, 6144], P('exp', 'ctx'), may hold values from -6 to 6
- decay_slopes: float32 [64], P('ctx'), may hold values from 0.0001 to 0.1
- residual: bfloat16 [512, 6144], P(('exp', 'ctx')), may hold values from -6 to 6
- mixer_gain: float32 [6144], replicated, may hold values from 0.25 to 1.75
- expert_gain: float32 [6144], replicated, may hold values from 0.25 to 1.75
- up_weight: bfloat16 [4, 9216, 6144], P('exp', 'ctx'), may hold values from -0.078125 to 0.078125
- down_weight: bfloat16 [4, 9216, 6144], P('exp', 'ctx'), may hold values from -0.0625 to 0.0625
- expert_ids: int32 [512, 2], P('exp'), may hold values from 0 to 3, all different within a row; in each aligned block of 128 rows (0 to 127, 128 to 255, ...) at most 68 rows name the same one
- gate_code: int32 [512, 2], P('exp'), may hold values from 0 to 15
- cotangent: bfloat16 [512, 6144], P(('exp', 'ctx')), may hold values from -6 to 6
Outputs:
- layer_output: bfloat16 [512, 6144], P(('exp', 'ctx'))
- residual_grad: bfloat16 [512, 6144], P(('exp', 'ctx'))
- query_grad: bfloat16 [512, 6144], P('exp', 'ctx')
- key_grad: bfloat16 [512, 6144], P('exp', 'ctx')
- value_grad: bfloat16 [512, 6144], P('exp', 'ctx')
The draws below stay inside these ranges and needn't reach their ends.
Inputs may be any that keep to these rules, and one draw needn't show every extreme that they name: `expert_ids`: each row names two different experts; in each aligned block of 128 rows (one sequence block) no expert is named by more than 68 rows.
All inputs are finite; a program needn't handle non-finite values.
Results may differ from the reference program's by a relative error of at most 0.0095.
Values may be sent and summed in bfloat16 or wider, within the bound.
No kernel may reach another device: no remote copies, remote signals or barrier semaphores. Data moves between devices by JAX's collectives and lax.ppermute only.
A program may use at most 256 MiB of HBM per device.

```python
import math
import jax
import jax.numpy as jnp
import numpy as np
from jax import lax

D = 6144
HEADS = 64
HEAD_DIM = 96
HE = 9216
TOKC = 128
SEQ = 512
EXPERTS = 4
CAP = 68


def touch_ends(values, key, least, largest):
    index_at = [jax.random.randint(jax.random.fold_in(key, axis), (), 0, length) for axis, length in enumerate(values.shape)]
    main_axis = values.shape.index(max(values.shape))
    neighbour = index_at[:main_axis] + [(index_at[main_axis] + 1) % values.shape[main_axis]] + index_at[main_axis + 1:]
    return values.at[tuple(index_at)].set(least).at[tuple(neighbour)].set(largest)


def level_of(stream_key, shape, pieces, smallest, top_value):
    level, own = 1.0, jax.random.fold_in(stream_key, 6)
    for axis_at, parts in pieces:
        draws = jnp.exp(jax.random.uniform(jax.random.fold_in(own, axis_at), (parts,), jnp.float32, smallest / len(pieces), top_value / len(pieces)))
        level = level * jnp.repeat(draws, shape[axis_at] // parts).reshape([-1 if axis == axis_at else 1 for axis in range(len(shape))])
    return level


def deal_out(stream_key, own, number, rows, number_of, top, bound, skew):
    sequence = jax.random.permutation(stream_key, number_of)
    crowded, common = portions_of(number_of, rows * top, bound, skew, True), portions_of(number_of, rows * top, bound, skew, False)
    places = jnp.arange(number_of)

    def named(tallies, turn):
        used = int((tallies > 0).sum())
        fixed = max(1, used // 4)
        passed = fixed + (places - fixed + turn * (used - fixed)) % max(1, number_of - fixed)
        return jnp.zeros((number_of,), jnp.int32).at[sequence[jnp.where(places < fixed, places, passed)]].set(jnp.asarray(tallies, jnp.int32))

    tallies = jnp.where(number % 4 == 0, named(crowded, number // 4), named(common, number - number // 4 - 1))
    mixed = jax.random.permutation(jax.random.fold_in(own, 3), number_of)
    donor, sink = mixed[0:number_of // 2 * 2:2], mixed[1:number_of // 2 * 2:2]
    margin = jnp.minimum(tallies[donor] - 1, bound - tallies[sink]) // 2
    margin = jnp.where((donor == sequence[0]) | (sink == sequence[0]) | (tallies[sink] == 0), 0, jnp.maximum(margin, 0))
    passed = jax.random.randint(jax.random.fold_in(own, 4), (number_of // 2,), 0, 1 << 20) % (margin + 1)
    tallies = tallies.at[donor].add(-passed).at[sink].add(passed)
    labels = jnp.searchsorted(jnp.cumsum(tallies), jnp.arange(rows * top), side="right").astype(jnp.int32)
    listing = labels.reshape(top, rows).T
    listing = listing[jax.random.permutation(jax.random.fold_in(own, 1), rows)]
    turn = jax.random.randint(jax.random.fold_in(own, 2), (rows, 1), 0, top)
    return jnp.take_along_axis(listing, (jnp.arange(top)[None, :] + turn) % top, axis=1)


def portions_of(count, total, bound, skew, full):
    loads = [(1 << 20) // math.isqrt(grade ** skew) + 1 for grade in range(1, count + 1)]
    largest = bound if full else min(bound, max(-(-total // count), total * loads[0] // sum(loads)))
    least = 1 if total - largest >= count - 1 else 0
    counts, spare = [largest] + [least] * (count - 1), total - largest - least * (count - 1)
    while spare > 0:
        movable = [i for i in range(1, count) if counts[i] < largest] or [i for i in range(1, count) if counts[i] < bound]
        whole, remaining = sum([loads[i] for i in movable]), spare
        for i in movable:
            extra = min(bound - counts[i], max(1, remaining * loads[i] // whole), spare)
            counts[i] = counts[i] + extra
            spare = spare - extra
    return np.array(counts)


def gaussian(rng, extent, scale, limit, split=(), held_as=jnp.bfloat16):
    loudness = level_of(rng, extent, split, -0.22, 0.18) if split else 1.0
    values = jax.random.normal(rng, extent, jnp.float32) * scale * loudness
    return jnp.minimum(jnp.maximum(values, -limit), limit).astype(held_as)


def setup_inputs(seed: int = 0) -> dict:
    seeds = jax.random.split(jax.random.key(seed), 13)
    queries = gaussian(seeds[0], (SEQ, D), 0.3, 4.0, ((0, 4), (1, 8)))
    key_vectors = gaussian(seeds[1], (SEQ, D), 0.3, 4.0, ((0, 4), (1, 8)))
    value_vectors = gaussian(seeds[2], (SEQ, D), 1.0, 6.0, ((0, 4), (1, 8)))
    decay_slopes = jnp.clip(jnp.exp(math.log(0.1) - 6.9077553 * jax.random.uniform(seeds[3], (HEADS,), jnp.float32) ** level_of(seeds[3], (HEADS,), ((0, 8),), -0.2, 0.2)), 0.0001, 0.1)
    residual = gaussian(seeds[4], (SEQ, D), 1.0, 6.0, ((0, 32),))
    mixer_gain = jnp.clip(1.0 + 0.15 * jax.random.normal(seeds[5], (D,), jnp.float32), 0.25, 1.75)
    expert_gain = jnp.clip(1.0 + 0.15 * jax.random.normal(seeds[6], (D,), jnp.float32), 0.25, 1.75)
    up_weight = gaussian(seeds[7], (EXPERTS, HE, D), D ** -0.5, 0.078125, ((0, 4), (1, 8)))
    down_weight = gaussian(seeds[8], (EXPERTS, HE, D), HE ** -0.5, 0.0625, ((0, 4), (1, 8)))
    expert_ids_keys = jax.random.split(jax.random.fold_in(seeds[9], 1), SEQ // TOKC)
    expert_ids_turns = jax.random.permutation(jax.random.fold_in(seeds[9], 3), SEQ // TOKC)
    expert_ids = jax.vmap(lambda own, number: deal_out(jax.random.fold_in(seeds[9], 2), own, number, TOKC, EXPERTS, 2, CAP, 2))(expert_ids_keys, expert_ids_turns).reshape((SEQ, 2))
    gate_code = touch_ends(jax.random.randint(seeds[10], (SEQ, 2), 0, 16), jax.random.fold_in(seeds[10], 1), 0, 15).astype(jnp.int32)
    cotangent = gaussian(seeds[11], (SEQ, D), 1.0, 6.0, ((0, 32),))
    return dict(queries=queries, key_vectors=key_vectors, value_vectors=value_vectors, decay_slopes=decay_slopes, residual=residual, mixer_gain=mixer_gain, expert_gain=expert_gain, up_weight=up_weight, down_weight=down_weight, expert_ids=expert_ids, gate_code=gate_code, cotangent=cotangent)


EPSILON = 1e-06
HIGHEST = lax.Precision.HIGHEST

def rms_gain(values, gain):
    return values * lax.rsqrt(lax.optimization_barrier(jnp.mean(values * values, axis=-1, keepdims=True)) + EPSILON) * gain

def span_output(query_rows, key_rows, value_rows, entering, slope):
    length = query_rows.shape[0]
    places = jnp.arange(length).astype(jnp.float32)
    spacing = places[:, None] - places[None, :]
    fading = jnp.where(spacing >= 0.0, jnp.exp(-slope * jnp.maximum(spacing, 0.0)), 0.0)
    scores = jnp.dot(query_rows, key_rows.T, preferred_element_type=jnp.float32)
    weights = (scores * fading).astype(jnp.bfloat16)
    inner = jnp.dot(weights, value_rows, preferred_element_type=jnp.float32)
    carried = jnp.dot(query_rows.astype(jnp.float32), entering, precision=HIGHEST)
    return inner + carried * jnp.exp(-slope * (places + 1.0))[:, None]

def span_summary(key_rows, value_rows, slope):
    length = key_rows.shape[0]
    places = jnp.arange(length).astype(jnp.float32)
    faded = key_rows.astype(jnp.float32) * jnp.exp(-slope * (length - 1.0 - places))[:, None]
    return jnp.dot(faded.T, value_rows.astype(jnp.float32), precision=HIGHEST)

def span_pair(query_rows, key_rows, value_rows, entering, slope):
    return (span_output(query_rows, key_rows, value_rows, entering, slope), span_summary(key_rows, value_rows, slope))

def state_grad(query_rows, grad_rows, slope):
    length = query_rows.shape[0]
    places = jnp.arange(length).astype(jnp.float32)
    faded = query_rows.astype(jnp.float32) * jnp.exp(-slope * (places + 1.0))[:, None]
    return jnp.dot(faded.T, grad_rows.astype(jnp.float32), precision=HIGHEST)

def span_backward(query_rows, key_rows, value_rows, entering, slope, grad_rows, grad_state):

    def local_pair(first, second, third):
        return span_pair(first, second, third, entering, slope)
    _, pullback = jax.vjp(local_pair, query_rows, key_rows, value_rows)
    return pullback((grad_rows.astype(jnp.float32), grad_state))

def silu_slope(before):
    sigma = jax.nn.sigmoid(before)
    return sigma * (1.0 + before * (1.0 - sigma))

def reference(queries, key_vectors, value_vectors, decay_slopes, residual, mixer_gain, expert_gain, up_weight, down_weight, expert_ids, gate_code, cotangent):
    blocks = SEQ // TOKC

    def split_heads(array):
        return array.reshape(blocks, TOKC, HEADS, HEAD_DIM)
    query_blocks = split_heads(queries)
    key_blocks = split_heads(key_vectors)
    value_blocks = split_heads(value_vectors)
    many_output = jax.vmap(span_output, in_axes=(1, 1, 1, 0, 0), out_axes=1)
    many_summary = jax.vmap(span_summary, in_axes=(1, 1, 0))
    many_grad = jax.vmap(state_grad, in_axes=(1, 1, 0))
    many_backward = jax.vmap(span_backward, in_axes=(1, 1, 1, 0, 0, 1, 0), out_axes=1)
    block_fade = jnp.exp(-decay_slopes * TOKC)[:, None, None]
    empty_state = jnp.zeros((HEADS, HEAD_DIM, HEAD_DIM), jnp.float32)

    def forward_step(state, block):
        query_rows, key_rows, value_rows = block
        mixed_rows = many_output(query_rows, key_rows, value_rows, state, decay_slopes).astype(jnp.bfloat16)
        return (block_fade * state + many_summary(key_rows, value_rows, decay_slopes), (mixed_rows, state))
    _, (mixed_blocks, entering) = lax.scan(forward_step, empty_state, (query_blocks, key_blocks, value_blocks))
    mixed = mixed_blocks.reshape(SEQ, D).astype(jnp.float32)
    hidden_low = (residual.astype(jnp.float32) + rms_gain(mixed, mixer_gain)).astype(jnp.bfloat16)
    hidden = lax.optimization_barrier(hidden_low).astype(jnp.float32)
    normed = rms_gain(hidden, expert_gain).astype(jnp.bfloat16)
    flat = expert_ids.reshape(blocks, 2 * TOKC).astype(jnp.int32)
    marks = (flat[:, :, None] == jnp.arange(EXPERTS, dtype=jnp.int32)[None, None, :]).astype(jnp.int32)
    slots = lax.optimization_barrier(jnp.sum((jnp.cumsum(marks, axis=1) - marks) * marks, axis=2)).astype(jnp.int32)
    share = ((1.0 + gate_code.astype(jnp.float32)) / 16.0).reshape(blocks, 2 * TOKC)
    sources = jnp.repeat(normed.reshape(blocks, TOKC, D), 2, axis=1)
    scaled = (jnp.repeat(cotangent.astype(jnp.float32).reshape(blocks, TOKC, D), 2, axis=1) * share[:, :, None]).astype(jnp.bfloat16)
    block_index = jnp.broadcast_to(jnp.arange(blocks, dtype=jnp.int32)[:, None], (blocks, 2 * TOKC))
    buffer_in = jnp.zeros((EXPERTS, blocks, CAP, D), jnp.bfloat16).at[flat, block_index, slots].set(sources)
    buffer_grad = jnp.zeros((EXPERTS, blocks, CAP, D), jnp.bfloat16).at[flat, block_index, slots].set(scaled)

    def expert_work(item):
        rows, grads, upward, downward = item
        rows = rows.reshape(blocks * CAP, D)
        grads = grads.reshape(blocks * CAP, D)
        before = jnp.dot(rows, upward.T, preferred_element_type=jnp.float32)
        active = jax.nn.silu(before).astype(jnp.bfloat16)
        result = jnp.dot(active, downward, preferred_element_type=jnp.float32).astype(jnp.bfloat16)
        backward = jnp.dot(grads, downward.T, preferred_element_type=jnp.float32)
        inner_grad = (backward * silu_slope(before)).astype(jnp.bfloat16)
        input_grad = jnp.dot(inner_grad, upward, preferred_element_type=jnp.float32).astype(jnp.bfloat16)
        return (result.reshape(blocks, CAP, D), input_grad.reshape(blocks, CAP, D))
    results, inputs = lax.map(expert_work, (buffer_in, buffer_grad, up_weight, down_weight))
    route_result = results[flat, block_index, slots].astype(jnp.float32)
    route_grad = inputs[flat, block_index, slots].astype(jnp.float32)
    combined = lax.optimization_barrier(jnp.sum((route_result * share[:, :, None]).reshape(blocks, TOKC, 2, D), axis=2)).reshape(SEQ, D)
    collected = lax.optimization_barrier(jnp.sum(route_grad.reshape(blocks, TOKC, 2, D), axis=2)).reshape(SEQ, D)
    layer_output = (hidden + combined).astype(jnp.bfloat16)
    _, pull_expert = jax.vjp(lambda values: rms_gain(values, expert_gain), hidden)
    hidden_grad = cotangent.astype(jnp.float32) + pull_expert(collected)[0]
    residual_grad = hidden_grad.astype(jnp.bfloat16)
    _, pull_mixer = jax.vjp(lambda values: rms_gain(values, mixer_gain), mixed)
    mixed_grad = pull_mixer(hidden_grad)[0].astype(jnp.bfloat16)
    grad_blocks = split_heads(mixed_grad)

    def backward_step(later, block):
        query_rows, key_rows, value_rows, state, grad_rows = block
        grads = many_backward(query_rows, key_rows, value_rows, state, decay_slopes, grad_rows, later)
        return (block_fade * later + many_grad(query_rows, grad_rows, decay_slopes), grads)
    _, (query_grad, key_grad, value_grad) = lax.scan(backward_step, empty_state, (query_blocks, key_blocks, value_blocks, entering, grad_blocks), reverse=True)
    return (layer_output, residual_grad, query_grad.reshape(SEQ, D), key_grad.reshape(SEQ, D), value_grad.reshape(SEQ, D))
```

```python
import jax
import jax.numpy as jnp
from jax import lax
from jax.sharding import PartitionSpec as P

EPSILON = 1e-06
HIGHEST = lax.Precision.HIGHEST
BF16 = jnp.bfloat16
F32 = jnp.float32


def span_output(query_rows, key_rows, value_rows, entering, slope):
    length = query_rows.shape[0]
    places = jnp.arange(length).astype(jnp.float32)
    spacing = places[:, None] - places[None, :]
    fading = jnp.where(spacing >= 0.0, jnp.exp(-slope * jnp.maximum(spacing, 0.0)), 0.0)
    scores = jnp.dot(query_rows, key_rows.T, preferred_element_type=jnp.float32)
    weights = (scores * fading).astype(jnp.bfloat16)
    inner = jnp.dot(weights, value_rows, preferred_element_type=jnp.float32)
    carried = jnp.dot(query_rows.astype(jnp.float32), entering, precision=HIGHEST)
    return inner + carried * jnp.exp(-slope * (places + 1.0))[:, None]


def span_summary(key_rows, value_rows, slope):
    length = key_rows.shape[0]
    places = jnp.arange(length).astype(jnp.float32)
    faded = key_rows.astype(jnp.float32) * jnp.exp(-slope * (length - 1.0 - places))[:, None]
    return jnp.dot(faded.T, value_rows.astype(jnp.float32), precision=HIGHEST)


def span_pair(query_rows, key_rows, value_rows, entering, slope):
    return (
        span_output(query_rows, key_rows, value_rows, entering, slope),
        span_summary(key_rows, value_rows, slope),
    )


def state_grad(query_rows, grad_rows, slope):
    length = query_rows.shape[0]
    places = jnp.arange(length).astype(jnp.float32)
    faded = query_rows.astype(jnp.float32) * jnp.exp(-slope * (places + 1.0))[:, None]
    return jnp.dot(faded.T, grad_rows.astype(jnp.float32), precision=HIGHEST)


def span_backward(query_rows, key_rows, value_rows, entering, slope, grad_rows, grad_state):

    def local_pair(first, second, third):
        return span_pair(first, second, third, entering, slope)

    _, pullback = jax.vjp(local_pair, query_rows, key_rows, value_rows)
    return pullback((grad_rows.astype(jnp.float32), grad_state))


def silu_slope(before):
    sigma = jax.nn.sigmoid(before)
    return sigma * (1.0 + before * (1.0 - sigma))


def ring_order(size):
    if size == 8:
        return [0, 2, 4, 6, 7, 5, 3, 1]
    return list(range(size))


class Ring:
    def __init__(self):
        self.size = lax.axis_size("ctx")
        order = ring_order(self.size)
        self.right = [(order[i], order[(i + 1) % self.size]) for i in range(self.size)]
        self.left = [(b, a) for a, b in self.right]
        place = [order.index(i) for i in range(self.size)]
        self.order = jnp.array(order, jnp.int32)
        self.place = jnp.array(place, jnp.int32)[lax.axis_index("ctx")]

    def at(self, offset):
        return self.order[(self.place + offset) % self.size]

    def go_right(self, x):
        return lax.ppermute(x, "ctx", self.right)

    def go_left(self, x):
        return lax.ppermute(x, "ctx", self.left)


def swap(x, k):
    return lax.ppermute(x, "exp", [(i, i ^ k) for i in range(lax.axis_size("exp"))])


def ctx_sum(x):
    size = lax.axis_size("ctx")
    step = 1
    while step < size:
        x = x + lax.ppermute(x, "ctx", [(i, i ^ step) for i in range(size)])
        step *= 2
    return x


def gather_all(x, ring):
    def spread(own):
        across = swap(own, 2)
        return [own, swap(own, 1), across, swap(across, 1)]

    found = [(0, spread(x))]
    to_right = to_left = x
    for step in range(1, ring.size // 2 + 1):
        to_right = ring.go_right(to_right)
        found.append((-step, spread(to_right)))
        if step < ring.size // 2:
            to_left = ring.go_left(to_left)
            found.append((step, spread(to_left)))
    return found


def reduce_to_owner(partial, ring):
    half = ring.size // 2
    far = partial(half)
    rows = far.shape[0]
    low = far.astype(BF16)
    to_right, to_left = low[: rows // 2], low[rows // 2 :]
    blank = jnp.zeros_like(to_right)
    to_right = jnp.concatenate([ring.go_right(to_right), blank], axis=0)
    to_left = jnp.concatenate([blank, ring.go_left(to_left)], axis=0)
    for offset in range(half - 1, 0, -1):
        to_right = ring.go_right((partial(offset) + to_right.astype(F32)).astype(BF16))
        to_left = ring.go_left((partial(-offset) + to_left.astype(F32)).astype(BF16))
    return partial(0) + to_right.astype(F32) + to_left.astype(F32)


def exclusive_count(marks):
    length = marks.shape[-1]
    earlier = (jnp.arange(length)[:, None] < jnp.arange(length)[None, :]).astype(BF16)
    return jnp.dot(marks, earlier, preferred_element_type=F32).astype(jnp.int32)


def fast_device(
    queries,
    key_vectors,
    value_vectors,
    decay_slopes,
    residual,
    mixer_gain,
    expert_gain,
    up_weight,
    down_weight,
    expert_ids,
    gate_code,
    cotangent,
):
    length, width = queries.shape
    features = residual.shape[1]
    local_heads = decay_slopes.shape[0]
    head_width = width // local_heads
    groups = lax.axis_size("exp")
    capacity = min(length, max(2, 17 * length // (8 * groups)))
    ring = Ring()
    here, mine = lax.axis_index("ctx"), lax.axis_index("exp")
    core = mine % 2

    both = jnp.concatenate([residual, cotangent], axis=0)
    both = lax.all_to_all(both, "ctx", split_axis=1, concat_axis=0, tiled=True)
    both = both.reshape(ring.size, 2, -1, width)
    residual_part = both[:, 0].reshape(length, width)
    cot_part = both[:, 1].reshape(length, width)
    cot_found = gather_all(cot_part, ring)

    codes = (expert_ids * 16 + gate_code).astype(F32)
    relative = [codes] + [swap(codes, j) for j in range(1, groups)]
    ids_near = jnp.stack(relative).astype(jnp.int32)
    ids_near, code_near = ids_near // 16, ids_near % 16
    hit = ids_near == mine
    taken = jnp.any(hit, axis=-1)
    share_near = jnp.sum(jnp.where(hit, (1.0 + code_near.astype(F32)) / 16.0, 0.0), axis=-1)
    slot_near = exclusive_count(taken.astype(BF16))
    row_near = slot_near + capacity * jnp.arange(groups, dtype=jnp.int32)[:, None]
    row_near = jnp.where(taken, row_near, -1).reshape(-1)
    pick = row_near[None, :] == jnp.arange(groups * capacity, dtype=jnp.int32)[:, None]
    pick_rows = pick.astype(BF16)
    pick_grads = jnp.where(pick, share_near.reshape(-1)[None, :], 0.0).astype(BF16)
    own_hit = expert_ids[None, :, :] == (mine ^ jnp.arange(groups, dtype=jnp.int32))[:, None, None]
    own_taken = jnp.any(own_hit, axis=-1)
    own_share = jnp.sum(
        jnp.where(own_hit, (1.0 + gate_code.astype(F32)) / 16.0, 0.0), axis=-1
    )
    own_row = exclusive_count(own_taken.astype(BF16))
    own_row = own_row + capacity * jnp.arange(groups, dtype=jnp.int32)[:, None]
    own_row = jnp.where(own_taken, own_row, -1)
    place = own_row[:, :, None] == jnp.arange(groups * capacity, dtype=jnp.int32)
    give_grad = jnp.any(place, axis=0).astype(BF16)
    give_out = jnp.sum(jnp.where(place, own_share[:, :, None], 0.0), axis=0).astype(BF16)

    query_heads = queries.reshape(length, local_heads, head_width)
    key_heads = key_vectors.reshape(length, local_heads, head_width)
    value_heads = value_vectors.reshape(length, local_heads, head_width)
    fade = jnp.exp(-decay_slopes * length)[:, None, None]
    summary = jax.vmap(span_summary, in_axes=(1, 1, 0))(key_heads, value_heads, decay_slopes)
    other = swap(summary, 1)
    pair = jnp.where(core == 0, fade * summary + other, fade * other + summary)
    before_pair = lax.ppermute(pair, "exp", [(0, 2), (1, 3)])
    entering = jnp.where(core == 0, before_pair, fade * before_pair + other)
    mixed_heads = jax.vmap(span_output, in_axes=(1, 1, 1, 0, 0), out_axes=1)(
        query_heads, key_heads, value_heads, entering, decay_slopes
    )
    mixed_low = lax.optimization_barrier(mixed_heads.reshape(length, width).astype(BF16))
    mixed = mixed_low.astype(F32)
    mix_gain = lax.dynamic_slice(mixer_gain, (here * width,), (width,))
    exp_gain = lax.dynamic_slice(expert_gain, (here * width,), (width,))
    mixed_square = ctx_sum(jnp.sum(mixed * mixed, axis=-1)[None])[0][:, None]
    scale_1 = lax.rsqrt(mixed_square / features + EPSILON)
    hidden_low = (residual_part.astype(F32) + mixed * scale_1 * mix_gain).astype(BF16)
    hidden_low = lax.optimization_barrier(hidden_low)
    hidden = hidden_low.astype(F32)
    hidden_found = gather_all(hidden_low, ring)
    cot = cot_part.astype(F32)
    early = jnp.stack(
        [
            jnp.sum(hidden * hidden, axis=-1),
            jnp.sum(mix_gain * mixed * cot, axis=-1),
            jnp.sum(mix_gain * mixed * hidden, axis=-1),
        ]
    )
    early = ctx_sum(early)

    up_hidden, down_hidden = up_weight[0], down_weight[0]
    hidden_slice = up_hidden.shape[0]

    def columns(weight, offset):
        return lax.dynamic_slice(weight, (0, ring.at(offset) * width), (hidden_slice, width))

    backward = 0.0
    for offset, pieces in cot_found:
        rows = jnp.dot(pick_grads, jnp.concatenate(pieces, axis=0), preferred_element_type=F32)
        backward += lax.dot_general(
            rows.astype(BF16),
            columns(down_hidden, offset),
            (((1,), (1,)), ((), ())),
            preferred_element_type=F32,
        )
    before, square = 0.0, 0.0
    for offset, pieces in hidden_found:
        rows = jnp.dot(pick_rows, jnp.concatenate(pieces, axis=0), preferred_element_type=F32)
        square += jnp.sum(rows * rows, axis=-1, keepdims=True)
        gain = lax.dynamic_slice(expert_gain, (ring.at(offset) * width,), (width,))
        before += lax.dot_general(
            (rows * gain).astype(BF16),
            columns(up_hidden, offset),
            (((1,), (1,)), ((), ())),
            preferred_element_type=F32,
        )
    before = before * lax.rsqrt(square / features + EPSILON)
    active = jax.nn.silu(before).astype(BF16)
    inner_grad = (backward * silu_slope(before)).astype(BF16)

    def combined_part(left, weight, give):
        def part(offset):
            rows = jnp.dot(left, columns(weight, offset), preferred_element_type=F32)
            rows = rows.astype(BF16).reshape(groups, capacity, width)
            rows = [rows[0]] + [swap(rows[j], j) for j in range(1, groups)]
            return jnp.dot(give, jnp.concatenate(rows, axis=0), preferred_element_type=F32)

        return part

    collected = reduce_to_owner(combined_part(inner_grad, up_hidden, give_grad), ring)
    combined = reduce_to_owner(combined_part(active, down_hidden, give_out), ring)

    scale_2 = lax.rsqrt(early[0][:, None] / features + EPSILON)
    gained = exp_gain * collected
    late = ctx_sum(
        jnp.stack(
            [jnp.sum(gained * hidden, axis=-1), jnp.sum(mix_gain * mixed * gained, axis=-1)]
        )
    )
    pull_2 = scale_2 * scale_2 * scale_2 / features * late[0][:, None]
    hidden_grad = cot + scale_2 * gained - hidden * pull_2
    along = early[1][:, None] + scale_2 * late[1][:, None] - pull_2 * early[2][:, None]
    mixed_grad = scale_1 * (mix_gain * hidden_grad) - mixed * (
        scale_1 * scale_1 * scale_1 / features * along
    )
    grad_heads = lax.optimization_barrier(mixed_grad.astype(BF16))
    grad_heads = grad_heads.reshape(length, local_heads, head_width)
    residual_grad = lax.all_to_all(
        hidden_grad.astype(BF16), "ctx", split_axis=0, concat_axis=1, tiled=True
    )
    layer_output = lax.all_to_all(
        (hidden + combined).astype(BF16), "ctx", split_axis=0, concat_axis=1, tiled=True
    )

    block_grad = jax.vmap(state_grad, in_axes=(1, 1, 0))(query_heads, grad_heads, decay_slopes)
    other = swap(block_grad, 1)
    pair = jnp.where(core == 0, block_grad + fade * other, other + fade * block_grad)
    after_pair = lax.ppermute(pair, "exp", [(2, 0), (3, 1)])
    later = jnp.where(core == 0, other + fade * after_pair, after_pair)
    query_grad, key_grad, value_grad = jax.vmap(
        span_backward, in_axes=(1, 1, 1, 0, 0, 1, 0), out_axes=1
    )(query_heads, key_heads, value_heads, entering, decay_slopes, grad_heads, later)
    return (
        layer_output,
        residual_grad,
        query_grad.reshape(length, -1),
        key_grad.reshape(length, -1),
        value_grad.reshape(length, -1),
    )


def entering_2(x, axis, combine, identity, reverse):
    count, position = (lax.axis_size(axis), lax.axis_index(axis))
    everything = jax.tree.map(lambda part: lax.all_gather(part, axis), x)
    start = jax.tree.map(
        lambda part, zero: jnp.broadcast_to(jnp.asarray(zero, part.dtype), part.shape), x, identity
    )

    def lap(k, before):
        at = count - 1 - k if reverse else k
        reached = at > position if reverse else at < position
        new = combine(before, jax.tree.map(lambda part: part[at], everything))
        return jax.tree.map(lambda a, b: jnp.where(reached, a, b), new, before)

    return lax.fori_loop(0, count, lap, start)


def rms_gain(values, gain):
    return values * lax.rsqrt(jnp.mean(values * values, axis=-1, keepdims=True) + EPSILON) * gain


def chain(earlier, later):
    return (earlier[0] * later[0], later[0][:, None, None] * earlier[1] + later[1])


def per_device(
    queries,
    key_vectors,
    value_vectors,
    decay_slopes,
    residual,
    mixer_gain,
    expert_gain,
    up_weight,
    down_weight,
    expert_ids,
    gate_code,
    cotangent,
):
    length = queries.shape[0]
    local_heads = decay_slopes.shape[0]
    head_width = queries.shape[1] // local_heads
    query_heads = queries.reshape(length, local_heads, head_width)
    key_heads = key_vectors.reshape(length, local_heads, head_width)
    value_heads = value_vectors.reshape(length, local_heads, head_width)
    block_fade = jnp.exp(-decay_slopes * length)
    summary = jax.vmap(span_summary, in_axes=(1, 1, 0))(key_heads, value_heads, decay_slopes)
    identity = (jnp.ones_like(block_fade), jnp.zeros_like(summary))
    entering = entering_2((block_fade, summary), "exp", chain, identity, False)[1]
    mixed_heads = jax.vmap(span_output, in_axes=(1, 1, 1, 0, 0), out_axes=1)(
        query_heads, key_heads, value_heads, entering, decay_slopes
    )
    mixed_heads = mixed_heads.astype(jnp.bfloat16).reshape(length, -1)
    mixed_low = lax.all_to_all(mixed_heads, "ctx", split_axis=0, concat_axis=1, tiled=True)
    mixed = mixed_low.astype(jnp.float32)
    hidden_low = (residual.astype(jnp.float32) + rms_gain(mixed, mixer_gain)).astype(jnp.bfloat16)
    hidden = lax.optimization_barrier(hidden_low).astype(jnp.float32)
    normed = rms_gain(hidden, expert_gain).astype(jnp.bfloat16)
    groups = lax.axis_size("exp")
    block_len = expert_ids.shape[0]
    capacity = min(block_len, max(2, 17 * block_len // (8 * groups)))
    share = ((1.0 + gate_code.astype(jnp.float32)) / 16.0).reshape(-1)
    flat = expert_ids.reshape(-1)
    marks = (flat[:, None] == jnp.arange(groups, dtype=jnp.int32)[None, :]).astype(jnp.int32)
    slots = jnp.sum((jnp.cumsum(marks, axis=0) - marks) * marks, axis=1)
    target = flat * capacity + slots
    matching = target[None, :] == jnp.arange(groups * capacity, dtype=jnp.int32)[:, None]
    filled = jnp.any(matching, axis=1)
    source_route = jnp.sum(
        jnp.where(matching, jnp.arange(2 * block_len, dtype=jnp.int32)[None, :], 0), axis=1
    )
    source_token = source_route // 2
    slot_share = jnp.take(share, source_route)
    up_hidden = up_weight[0]
    down_hidden = down_weight[0]
    block_normed, block_cot = (
        lax.all_gather(normed, "ctx", axis=0, tiled=True),
        lax.all_gather(cotangent, "ctx", axis=0, tiled=True),
    )
    taken = jnp.take(block_normed, source_token, axis=0)
    rows = jnp.where(filled[:, None], taken, jnp.zeros_like(taken))
    weighted = jnp.take(block_cot, source_token, axis=0).astype(jnp.float32) * slot_share[:, None]
    grads = jnp.where(filled[:, None], weighted, 0.0).astype(jnp.bfloat16)
    send_rows = rows.reshape(groups, capacity, -1)
    send_grad = grads.reshape(groups, capacity, -1)
    pieces = (
        lax.all_to_all(send_rows, "exp", split_axis=0, concat_axis=0, tiled=True),
        lax.all_to_all(send_grad, "exp", split_axis=0, concat_axis=0, tiled=True),
    )
    before = jnp.einsum("bsd,hd->bsh", pieces[0], up_hidden, preferred_element_type=jnp.float32)
    backward = jnp.einsum("bsd,hd->bsh", pieces[1], down_hidden, preferred_element_type=jnp.float32)
    before = before.reshape(-1, before.shape[-1])
    backward = backward.reshape(-1, backward.shape[-1])
    active = jax.nn.silu(before).astype(jnp.bfloat16)
    inner_grad = (backward * silu_slope(before)).astype(jnp.bfloat16)
    up_moved, down_moved = (
        lax.all_to_all(up_weight, "ctx", split_axis=2, concat_axis=1, tiled=True),
        lax.all_to_all(down_weight, "ctx", split_axis=2, concat_axis=1, tiled=True),
    )
    up_features = up_moved[0]
    down_features = down_moved[0]
    pieces = (
        lax.all_gather(active, "ctx", axis=1, tiled=True),
        lax.all_gather(inner_grad, "ctx", axis=1, tiled=True),
    )
    out_total = jnp.dot(pieces[0], down_features, preferred_element_type=jnp.float32)
    in_total = jnp.dot(pieces[1], up_features, preferred_element_type=jnp.float32)
    columns = down_features.shape[1]
    result = out_total.astype(jnp.bfloat16).reshape(groups, capacity, columns)
    input_grad = in_total.astype(jnp.bfloat16).reshape(groups, capacity, columns)
    back_rows, back_grad = (
        lax.all_to_all(result, "exp", split_axis=0, concat_axis=0, tiled=True),
        lax.all_to_all(input_grad, "exp", split_axis=0, concat_axis=0, tiled=True),
    )
    back_rows = back_rows.reshape(groups * capacity, columns)
    back_grad = back_grad.reshape(groups * capacity, columns)
    route_result = jnp.take(back_rows, target, axis=0).astype(jnp.float32)
    route_grad = jnp.take(back_grad, target, axis=0).astype(jnp.float32)
    combined = jnp.sum((route_result * share[:, None]).reshape(block_len, 2, columns), axis=1)
    collected = jnp.sum(route_grad.reshape(block_len, 2, columns), axis=1)
    combined_rows, collected_rows = (
        lax.all_to_all(combined, "ctx", split_axis=0, concat_axis=1, tiled=True),
        lax.all_to_all(collected, "ctx", split_axis=0, concat_axis=1, tiled=True),
    )
    layer_output = (hidden + combined_rows).astype(jnp.bfloat16)
    _, pull_expert = jax.vjp(lambda values: rms_gain(values, expert_gain), hidden)
    hidden_grad = cotangent.astype(jnp.float32) + pull_expert(collected_rows)[0]
    residual_grad = hidden_grad.astype(jnp.bfloat16)
    _, pull_mixer = jax.vjp(lambda values: rms_gain(values, mixer_gain), mixed)
    mixed_grad = pull_mixer(hidden_grad)[0].astype(jnp.bfloat16)
    grad_heads = lax.all_to_all(mixed_grad, "ctx", split_axis=1, concat_axis=0, tiled=True).reshape(
        length, local_heads, head_width
    )
    block_grad = jax.vmap(state_grad, in_axes=(1, 1, 0))(query_heads, grad_heads, decay_slopes)
    later = entering_2((block_fade, block_grad), "exp", chain, identity, True)[1]
    query_grad, key_grad, value_grad = jax.vmap(
        span_backward, in_axes=(1, 1, 1, 0, 0, 1, 0), out_axes=1
    )(query_heads, key_heads, value_heads, entering, decay_slopes, grad_heads, later)
    return (
        layer_output,
        residual_grad,
        query_grad.reshape(length, -1),
        key_grad.reshape(length, -1),
        value_grad.reshape(length, -1),
    )


def solution(mesh):
    in_specs = (
        P("exp", "ctx"),
        P("exp", "ctx"),
        P("exp", "ctx"),
        P("ctx"),
        P(("exp", "ctx"), None),
        P(),
        P(),
        P("exp", "ctx", None),
        P("exp", "ctx", None),
        P("exp", None),
        P("exp", None),
        P(("exp", "ctx"), None),
    )
    out_specs = (
        P(("exp", "ctx"), None),
        P(("exp", "ctx"), None),
        P("exp", "ctx"),
        P("exp", "ctx"),
        P("exp", "ctx"),
    )
    fast = mesh.shape["ctx"] == 8 and mesh.shape["exp"] == 4
    body = fast_device if fast else per_device
    return jax.shard_map(
        body, mesh=mesh, in_specs=in_specs, out_specs=out_specs, check_vma=False
    )
```

```python
import jax
import jax.numpy as jnp
from jax import lax
from jax.experimental import pallas as pl
from jax.experimental.pallas import tpu as pltpu
from jax.sharding import PartitionSpec as P

EPSILON = 1e-06
HIGHEST = lax.Precision.HIGHEST
BF16 = jnp.bfloat16
F32 = jnp.float32


def span_output(query_rows, key_rows, value_rows, entering, slope):
    length = query_rows.shape[0]
    places = jnp.arange(length).astype(jnp.float32)
    spacing = places[:, None] - places[None, :]
    fading = jnp.where(spacing >= 0.0, jnp.exp(-slope * jnp.maximum(spacing, 0.0)), 0.0)
    scores = jnp.dot(query_rows, key_rows.T, preferred_element_type=jnp.float32)
    weights = (scores * fading).astype(jnp.bfloat16)
    inner = jnp.dot(weights, value_rows, preferred_element_type=jnp.float32)
    carried = jnp.dot(query_rows.astype(jnp.float32), entering, precision=HIGHEST)
    return inner + carried * jnp.exp(-slope * (places + 1.0))[:, None]


def span_summary(key_rows, value_rows, slope):
    length = key_rows.shape[0]
    places = jnp.arange(length).astype(jnp.float32)
    faded = key_rows.astype(jnp.float32) * jnp.exp(-slope * (length - 1.0 - places))[:, None]
    return jnp.dot(faded.T, value_rows.astype(jnp.float32), precision=HIGHEST)


def span_pair(query_rows, key_rows, value_rows, entering, slope):
    return (
        span_output(query_rows, key_rows, value_rows, entering, slope),
        span_summary(key_rows, value_rows, slope),
    )


def state_grad(query_rows, grad_rows, slope):
    length = query_rows.shape[0]
    places = jnp.arange(length).astype(jnp.float32)
    faded = query_rows.astype(jnp.float32) * jnp.exp(-slope * (places + 1.0))[:, None]
    return jnp.dot(faded.T, grad_rows.astype(jnp.float32), precision=HIGHEST)


def span_backward(query_rows, key_rows, value_rows, entering, slope, grad_rows, grad_state):

    def local_pair(first, second, third):
        return span_pair(first, second, third, entering, slope)

    _, pullback = jax.vjp(local_pair, query_rows, key_rows, value_rows)
    return pullback((grad_rows.astype(jnp.float32), grad_state))


def silu_slope(before):
    sigma = jax.nn.sigmoid(before)
    return sigma * (1.0 + before * (1.0 - sigma))


def ring_order(size):
    if size == 8:
        return [0, 2, 4, 6, 7, 5, 3, 1]
    return list(range(size))


class Ring:
    def __init__(self):
        self.size = lax.axis_size("ctx")
        order = ring_order(self.size)
        self.right = [(order[i], order[(i + 1) % self.size]) for i in range(self.size)]
        self.left = [(b, a) for a, b in self.right]
        place = [order.index(i) for i in range(self.size)]
        self.order = jnp.array(order, jnp.int32)
        self.place = jnp.array(place, jnp.int32)[lax.axis_index("ctx")]

    def at(self, offset):
        return self.order[(self.place + offset) % self.size]

    def go_right(self, x):
        return lax.ppermute(x, "ctx", self.right)

    def go_left(self, x):
        return lax.ppermute(x, "ctx", self.left)


def swap(x, k):
    return lax.ppermute(x, "exp", [(i, i ^ k) for i in range(lax.axis_size("exp"))])


def ctx_sum(x):
    size = lax.axis_size("ctx")
    step = 1
    while step < size:
        x = x + lax.ppermute(x, "ctx", [(i, i ^ step) for i in range(size)])
        step *= 2
    return x


def ring_sum(partial, ring):
    far = partial[4]
    rows = far.shape[0]
    low = far.astype(BF16)
    to_right, to_left = low[: rows // 2], low[rows // 2 :]
    blank = jnp.zeros_like(to_right)
    to_right = jnp.concatenate([ring.go_right(to_right), blank], axis=0)
    to_left = jnp.concatenate([blank, ring.go_left(to_left)], axis=0)
    for offset in (3, 2, 1):
        to_right = ring.go_right((partial[offset] + to_right.astype(F32)).astype(BF16))
        to_left = ring.go_left((partial[-offset] + to_left.astype(F32)).astype(BF16))
    return partial[0] + to_right.astype(F32) + to_left.astype(F32)


def ring_block(size, offset):
    here = lax.axis_index("ctx")
    row, column = here // 2, here % 2
    place = row + column * (size - 1 - 2 * row)
    at = (place + offset + size) % size
    far = at // (size // 2)
    return 2 * at + far * (2 * size - 1 - 4 * at)


def columns(weight_ref, block, size):
    width = weight_ref.shape[1] // size
    return weight_ref[:, pl.ds(pl.multiple_of(block * width, width), width)]


WHOLE = pl.BlockSpec(memory_space=pltpu.VMEM)
ANYWHERE = pl.BlockSpec(memory_space=pl.ANY)
IN_HBM = pl.BlockSpec(memory_space=pltpu.HBM)
NT = (((1,), (1,)), ((), ()))


def cost(rows, hidden, width):
    return pl.CostEstimate(
        flops=2 * rows * hidden * width, bytes_accessed=2 * hidden * width, transcendentals=0
    )


def load_call(arrays, after=()):
    count = len(arrays)

    def kernel(*refs):
        sources, targets, arrived = refs[:count], refs[-1 - count : -1], refs[-1]
        copies = [
            pltpu.make_async_copy(source, target, arrived.at[k])
            for k, (source, target) in enumerate(zip(sources, targets))
        ]
        for copy in copies:
            copy.start()
        for copy in copies:
            copy.wait()

    return pl.pallas_call(
        kernel,
        in_specs=[IN_HBM] * count + [ANYWHERE] * len(after),
        out_specs=[WHOLE] * count,
        out_shape=[pltpu.VMEM(x.shape, x.dtype) for x in arrays],
        scratch_shapes=[pltpu.SemaphoreType.DMA((count,))],
        compiler_params=pltpu.CompilerParams(vmem_limit_bytes=32 * 2**20),
        name="load_weights",
    )(*arrays, *after)


def backward_call(rows_all, weight, before, share, after=()):
    rows, features = rows_all.shape
    hidden = weight.shape[0]
    span, parts = rows // 4, 4
    part = features // parts

    def kernel(rows_ref, weight_ref, before_ref, share_ref, *refs):
        out_ref, held, total, landed = refs[-4:]
        mine = lax.axis_index("exp")
        core, side = lax.rem(mine, 2), mine // 2

        def fetch(k):
            copies = []
            for j, (flip_side, flip_core) in enumerate(((0, 0), (1, 0), (0, 1), (1, 1))):
                block = 2 * (side + flip_side * (1 - 2 * side)) + core
                block = block + flip_core * (1 - 2 * core)
                copies.append(
                    pltpu.make_async_copy(
                        rows_ref.at[
                            pl.ds(pl.multiple_of(block * span, span), span),
                            pl.ds(k * part, part),
                        ],
                        held.at[k % 2, pl.ds(j * span, span), :],
                        landed.at[k % 2, j],
                    )
                )
                copies[-1].start()
            return copies

        coming = fetch(0)
        for k in range(parts):
            arrived = coming
            if k + 1 < parts:
                coming = fetch(k + 1)
            for copy in arrived:
                copy.wait()
            value = lax.dot_general(
                held[k % 2],
                weight_ref[:, pl.ds(k * part, part)],
                NT,
                preferred_element_type=F32,
            )
            total[...] = value if k == 0 else total[...] + value
        here, share = before_ref[...], share_ref[...]
        sigma = 1.0 / (1.0 + jnp.exp(-here))
        value = share * total[...] * (sigma * (1.0 + here * (1.0 - sigma)))
        out_ref[...] = jnp.where(share > 0.0, value, 0.0).astype(BF16)

    return pl.pallas_call(
        kernel,
        in_specs=[IN_HBM] + [WHOLE] * 3 + [ANYWHERE] * len(after),
        out_specs=WHOLE,
        out_shape=jax.ShapeDtypeStruct((rows, hidden), BF16),
        scratch_shapes=[
            pltpu.VMEM((2, rows, part), BF16),
            pltpu.VMEM((rows, hidden), F32),
            pltpu.SemaphoreType.DMA((2, 4)),
        ],
        compiler_params=pltpu.CompilerParams(vmem_limit_bytes=10 * 2**20),
        cost_estimate=cost(rows, hidden, features),
        name="backward_rows",
    )(rows_all, weight, before, share, *after)


def before_call(found, ring, offsets, weight, gain, start=None, share=None, after=()):
    count = len(offsets)
    pieces = [part for o in offsets for part in found[o]]
    half, width = pieces[0].shape
    rows, hidden, features, size = 2 * half, weight.shape[0], weight.shape[1], ring.size
    gain = gain.reshape(size, width)
    sums = [jax.ShapeDtypeStruct((rows, hidden), F32), jax.ShapeDtypeStruct((rows, 1), F32)]
    first, last = start is None, share is not None

    def kernel(weight_ref, gain_ref, *refs):
        refs = list(refs)
        parts = [refs.pop(0) for _ in pieces]
        begin = [] if first else [refs.pop(0), refs.pop(0)]
        share_ref = refs.pop(0) if last else None
        refs = refs[len(after) :]
        total, other = refs.pop(0), refs.pop(0)
        held, scaled, landed = refs[:3]
        copies = []
        for k in range(count):
            for side in range(2):
                copies.append(
                    pltpu.make_async_copy(
                        parts[2 * k + side],
                        held.at[k, pl.ds(side * half, half), :],
                        landed.at[2 * k + side],
                    )
                )
                copies[-1].start()
        square = None if first else begin[1][...]
        for k in range(count):
            copies[2 * k].wait()
            copies[2 * k + 1].wait()
            value = held[k].astype(F32)
            squares = jnp.sum(value * value, axis=-1, keepdims=True)
            square = squares if square is None else square + squares
            block = ring_block(size, offsets[k])
            scaled[...] = (value * gain_ref[pl.ds(block, 1), :]).astype(BF16)
            product = lax.dot_general(
                scaled[...], columns(weight_ref, block, size), NT, preferred_element_type=F32
            )
            if k == 0:
                total[...] = product if first else begin[0][...] + product
            else:
                total[...] += product
        if last:
            before = total[...] * lax.rsqrt(square / features + EPSILON)
            total[...] = before
            active = before * (1.0 / (1.0 + jnp.exp(-before)))
            other[...] = jnp.where(share_ref[...] > 0.0, active, 0.0).astype(BF16)
        else:
            other[...] = square

    rest = list(start or ()) + ([share] if last else [])
    return pl.pallas_call(
        kernel,
        in_specs=[WHOLE, WHOLE]
        + [ANYWHERE] * len(pieces)
        + [WHOLE] * len(rest)
        + [ANYWHERE] * len(after),
        out_specs=[WHOLE, WHOLE],
        out_shape=[sums[0], jax.ShapeDtypeStruct((rows, hidden), BF16) if last else sums[1]],
        scratch_shapes=[
            pltpu.VMEM((count, rows, width), BF16),
            pltpu.VMEM((rows, width), BF16),
            pltpu.SemaphoreType.DMA((2 * count,)),
        ],
        compiler_params=pltpu.CompilerParams(vmem_limit_bytes=8 * 2**20),
        cost_estimate=cost(rows, hidden, count * width),
        name="before_rows",
    )(weight, gain, *pieces, *rest, *after)


def second_call(left, ring, offsets, weight, share=None, after=()):
    count = len(offsets)
    rows, hidden = left.shape
    half, size = rows // 2, ring.size
    width = weight.shape[1] // size

    def kernel(weight_ref, left_ref, *refs):
        keep_ref, give_ref = refs[-2:]
        for k in range(count):
            block = ring_block(size, offsets[k])
            value = jnp.dot(
                left_ref[...], columns(weight_ref, block, size), preferred_element_type=F32
            )
            if share is not None:
                value = value * refs[0][...]
            keep_ref[k] = value[:half].astype(BF16)
            give_ref[k] = value[half:].astype(BF16)

    extra = [] if share is None else [share]
    return pl.pallas_call(
        kernel,
        in_specs=[WHOLE] * (2 + len(extra)) + [ANYWHERE] * len(after),
        out_specs=[WHOLE, WHOLE],
        out_shape=[jax.ShapeDtypeStruct((count, half, width), BF16)] * 2,
        compiler_params=pltpu.CompilerParams(vmem_limit_bytes=8 * 2**20),
        cost_estimate=cost(rows, hidden, count * width),
        name="partial_rows",
    )(weight, left, *extra, *after)


def turn_call(residual, cotangent, after, ring):
    rows, features = residual.shape
    width = features // ring.size

    def kernel(residual_ref, cotangent_ref, after_ref, out_ref):
        for k in range(ring.size):
            span = pl.ds(k * width, width)
            out_ref[k, pl.ds(0, rows), :] = residual_ref[:, span]
            out_ref[k, pl.ds(rows, rows), :] = cotangent_ref[:, span]

    return pl.pallas_call(
        kernel,
        in_specs=[WHOLE, WHOLE, ANYWHERE],
        out_specs=WHOLE,
        out_shape=jax.ShapeDtypeStruct((ring.size, 2 * rows, width), BF16),
        name="turn",
    )(residual, cotangent, after)


def fast_device(
    queries,
    key_vectors,
    value_vectors,
    decay_slopes,
    residual,
    mixer_gain,
    expert_gain,
    up_weight,
    down_weight,
    expert_ids,
    gate_code,
    cotangent,
):
    length, width = queries.shape
    features = residual.shape[1]
    local_heads = decay_slopes.shape[0]
    head_width = width // local_heads
    ring = Ring()
    here, mine = lax.axis_index("ctx"), lax.axis_index("exp")
    core = mine % 2

    cot_all = lax.all_gather(cotangent, ("exp", "ctx"), axis=0, tiled=True)

    codes = (expert_ids * 16 + gate_code).astype(F32)
    codes = jnp.concatenate([codes, swap(codes, 2)], axis=0)
    codes = jnp.concatenate([codes, swap(codes, 1)], axis=0).astype(jnp.int32)
    share = jnp.where(codes // 16 == mine, (1.0 + (codes % 16).astype(F32)) / 16.0, 0.0)
    share = jnp.sum(share, axis=-1, keepdims=True)

    query_heads = queries.reshape(length, local_heads, head_width)
    key_heads = key_vectors.reshape(length, local_heads, head_width)
    value_heads = value_vectors.reshape(length, local_heads, head_width)
    fade = jnp.exp(-decay_slopes * length)[:, None, None]
    summary = jax.vmap(span_summary, in_axes=(1, 1, 0))(key_heads, value_heads, decay_slopes)
    other = swap(summary, 1)
    pair = jnp.where(core == 0, fade * summary + other, fade * other + summary)
    both = turn_call(residual, cotangent, other, ring)
    both = lax.all_to_all(both, "ctx", split_axis=0, concat_axis=0, tiled=True)
    both = both.reshape(ring.size, 2, -1, width)
    residual_part = both[:, 0].reshape(length, width)
    cot_part = both[:, 1].reshape(length, width)
    before_pair = lax.ppermute(pair, "exp", [(0, 2), (1, 3)])
    entering = jnp.where(core == 0, before_pair, fade * before_pair + other)
    mixed_heads = jax.vmap(span_output, in_axes=(1, 1, 1, 0, 0), out_axes=1)(
        query_heads, key_heads, value_heads, entering, decay_slopes
    )
    mixed_low = lax.optimization_barrier(mixed_heads.reshape(length, width).astype(BF16))
    mixed = mixed_low.astype(F32)
    mix_gain = lax.dynamic_slice(mixer_gain, (here * width,), (width,))
    exp_gain = lax.dynamic_slice(expert_gain, (here * width,), (width,))
    mixed_square = ctx_sum(jnp.sum(mixed * mixed, axis=-1)[None])[0][:, None]
    scale_1 = lax.rsqrt(mixed_square / features + EPSILON)
    hidden_low = (residual_part.astype(F32) + mixed * scale_1 * mix_gain).astype(BF16)
    hidden_low = lax.optimization_barrier(hidden_low)
    hidden = hidden_low.astype(F32)
    across = swap(hidden_low, 2)
    rights, lefts = [hidden_low], [hidden_low]
    for step in range(1, 5):
        rights.append(ring.go_right(rights[-1]))
        if step < 4:
            lefts.append(ring.go_left(lefts[-1]))
    cot = cot_part.astype(F32)
    early = jnp.stack(
        [
            jnp.sum(hidden * hidden, axis=-1),
            jnp.sum(mix_gain * mixed * cot, axis=-1),
            jnp.sum(mix_gain * mixed * hidden, axis=-1),
        ]
    )

    up_hidden, down_hidden = load_call((up_weight[0], down_weight[0]), (across,))
    found = {}
    for step in range(5):
        for offset, rows in ((-step, rights), (step, lefts)):
            if (step < 4 and (step > 0 or rows is rights)) or (step == 4 and rows is rights):
                own = rows[step]
                own = jnp.concatenate([own, across if step == 0 else swap(own, 2)], axis=0)
                found[4 if step == 4 else offset] = (own, swap(own, 1))

    def before_part(offsets, sums=None, share=None, after=()):
        return before_call(found, ring, offsets, up_hidden, expert_gain, sums, share, after)

    sums = before_part((0,), after=(rights[3],))
    sums = before_part((-1, 1), sums, after=(rights[4],))
    sums = before_part((-2, 2), sums)
    sums = before_part((-3, 3), sums)
    before, active = before_part((4,), sums, share)

    in_parts, out_parts = {}, {}

    def second(left, offsets, weight, parts, scale, after):
        keep, give = second_call(left, ring, offsets, weight, scale, after)
        got = swap(give, 1)
        for i, offset in enumerate(offsets):
            parts[offset] = keep[i].astype(F32) + got[i].astype(F32)
        return give, got

    def second_in(offsets, *after):
        return second(inner_grad, offsets, up_hidden, in_parts, None, after)

    def second_out(offsets, *after):
        return second(active, offsets, down_hidden, out_parts, share, after)

    def cross(offsets):
        far = jnp.stack([in_parts[o][length:].astype(BF16) for o in offsets])
        far = swap(far, 2)
        for i, o in enumerate(offsets):
            in_parts[o] = in_parts[o][:length] + far[i].astype(F32)
        return far

    give, got_a = second_out((4,))
    give, got_b = second_out((3, -3), give)
    inner_grad = backward_call(cot_all, down_hidden, before, share, (give, got_a))
    give, got_c = second_in((4,))
    far_0 = cross((4,))
    give, got_d = second_in((3, -3), give, got_b)
    far_1 = cross((3, -3))
    give, got_e = second_out((2, -2), give, got_c)
    give, got_f = second_in((2, -2), give, got_d)
    cross((2, -2))
    give, _ = second_out((1, -1), give, got_e, far_0)
    give, got_g = second_in((1, -1), give, got_f)
    cross((1, -1))
    give, _ = second_out((0,), give, far_1)
    second_in((0,), give, got_g)
    cross((0,))
    collected = ring_sum(in_parts, ring)
    combined = ring_sum(out_parts, ring)
    combined = combined[:length] + swap(combined[length:].astype(BF16), 2).astype(F32)

    gained = exp_gain * collected
    late = jnp.stack(
        [jnp.sum(gained * hidden, axis=-1), jnp.sum(mix_gain * mixed * gained, axis=-1)]
    )
    hidden_square, along_cot, along_hidden, along_gained, along_mixed = ctx_sum(
        jnp.concatenate([early, late], axis=0)
    )[:, :, None]
    scale_2 = lax.rsqrt(hidden_square / features + EPSILON)
    pull_2 = scale_2 * scale_2 * scale_2 / features * along_gained
    hidden_grad = cot + scale_2 * gained - hidden * pull_2
    along = along_cot + scale_2 * along_mixed - pull_2 * along_hidden
    mixed_grad = scale_1 * (mix_gain * hidden_grad) - mixed * (
        scale_1 * scale_1 * scale_1 / features * along
    )
    grad_heads = lax.optimization_barrier(mixed_grad.astype(BF16))
    grad_heads = grad_heads.reshape(length, local_heads, head_width)
    ends = jnp.concatenate(
        [x.astype(BF16).reshape(ring.size, -1, width) for x in (hidden_grad, hidden + combined)],
        axis=1,
    )
    ends = lax.all_to_all(ends, "ctx", split_axis=0, concat_axis=0, tiled=True)
    ends = ends.transpose(1, 0, 2).reshape(2, -1, features)
    residual_grad, layer_output = ends[0], ends[1]

    block_grad = jax.vmap(state_grad, in_axes=(1, 1, 0))(query_heads, grad_heads, decay_slopes)
    other = swap(block_grad, 1)
    pair = jnp.where(core == 0, block_grad + fade * other, other + fade * block_grad)
    after_pair = lax.ppermute(pair, "exp", [(2, 0), (3, 1)])
    later = jnp.where(core == 0, other + fade * after_pair, after_pair)
    query_grad, key_grad, value_grad = jax.vmap(
        span_backward, in_axes=(1, 1, 1, 0, 0, 1, 0), out_axes=1
    )(query_heads, key_heads, value_heads, entering, decay_slopes, grad_heads, later)
    return (
        layer_output,
        residual_grad,
        query_grad.reshape(length, -1),
        key_grad.reshape(length, -1),
        value_grad.reshape(length, -1),
    )


def entering_2(x, axis, combine, identity, reverse):
    count, position = (lax.axis_size(axis), lax.axis_index(axis))
    everything = jax.tree.map(lambda part: lax.all_gather(part, axis), x)
    start = jax.tree.map(
        lambda part, zero: jnp.broadcast_to(jnp.asarray(zero, part.dtype), part.shape), x, identity
    )

    def lap(k, before):
        at = count - 1 - k if reverse else k
        reached = at > position if reverse else at < position
        new = combine(before, jax.tree.map(lambda part: part[at], everything))
        return jax.tree.map(lambda a, b: jnp.where(reached, a, b), new, before)

    return lax.fori_loop(0, count, lap, start)


def rms_gain(values, gain):
    return values * lax.rsqrt(jnp.mean(values * values, axis=-1, keepdims=True) + EPSILON) * gain


def chain(earlier, later):
    return (earlier[0] * later[0], later[0][:, None, None] * earlier[1] + later[1])


def per_device(
    queries,
    key_vectors,
    value_vectors,
    decay_slopes,
    residual,
    mixer_gain,
    expert_gain,
    up_weight,
    down_weight,
    expert_ids,
    gate_code,
    cotangent,
):
    length = queries.shape[0]
    local_heads = decay_slopes.shape[0]
    head_width = queries.shape[1] // local_heads
    query_heads = queries.reshape(length, local_heads, head_width)
    key_heads = key_vectors.reshape(length, local_heads, head_width)
    value_heads = value_vectors.reshape(length, local_heads, head_width)
    block_fade = jnp.exp(-decay_slopes * length)
    summary = jax.vmap(span_summary, in_axes=(1, 1, 0))(key_heads, value_heads, decay_slopes)
    identity = (jnp.ones_like(block_fade), jnp.zeros_like(summary))
    entering = entering_2((block_fade, summary), "exp", chain, identity, False)[1]
    mixed_heads = jax.vmap(span_output, in_axes=(1, 1, 1, 0, 0), out_axes=1)(
        query_heads, key_heads, value_heads, entering, decay_slopes
    )
    mixed_heads = mixed_heads.astype(jnp.bfloat16).reshape(length, -1)
    mixed_low = lax.all_to_all(mixed_heads, "ctx", split_axis=0, concat_axis=1, tiled=True)
    mixed = mixed_low.astype(jnp.float32)
    hidden_low = (residual.astype(jnp.float32) + rms_gain(mixed, mixer_gain)).astype(jnp.bfloat16)
    hidden = lax.optimization_barrier(hidden_low).astype(jnp.float32)
    normed = rms_gain(hidden, expert_gain).astype(jnp.bfloat16)
    groups = lax.axis_size("exp")
    block_len = expert_ids.shape[0]
    capacity = min(block_len, max(2, 17 * block_len // (8 * groups)))
    share = ((1.0 + gate_code.astype(jnp.float32)) / 16.0).reshape(-1)
    flat = expert_ids.reshape(-1)
    marks = (flat[:, None] == jnp.arange(groups, dtype=jnp.int32)[None, :]).astype(jnp.int32)
    slots = jnp.sum((jnp.cumsum(marks, axis=0) - marks) * marks, axis=1)
    target = flat * capacity + slots
    matching = target[None, :] == jnp.arange(groups * capacity, dtype=jnp.int32)[:, None]
    filled = jnp.any(matching, axis=1)
    source_route = jnp.sum(
        jnp.where(matching, jnp.arange(2 * block_len, dtype=jnp.int32)[None, :], 0), axis=1
    )
    source_token = source_route // 2
    slot_share = jnp.take(share, source_route)
    up_hidden = up_weight[0]
    down_hidden = down_weight[0]
    block_normed, block_cot = (
        lax.all_gather(normed, "ctx", axis=0, tiled=True),
        lax.all_gather(cotangent, "ctx", axis=0, tiled=True),
    )
    taken = jnp.take(block_normed, source_token, axis=0)
    rows = jnp.where(filled[:, None], taken, jnp.zeros_like(taken))
    weighted = jnp.take(block_cot, source_token, axis=0).astype(jnp.float32) * slot_share[:, None]
    grads = jnp.where(filled[:, None], weighted, 0.0).astype(jnp.bfloat16)
    send_rows = rows.reshape(groups, capacity, -1)
    send_grad = grads.reshape(groups, capacity, -1)
    pieces = (
        lax.all_to_all(send_rows, "exp", split_axis=0, concat_axis=0, tiled=True),
        lax.all_to_all(send_grad, "exp", split_axis=0, concat_axis=0, tiled=True),
    )
    before = jnp.einsum("bsd,hd->bsh", pieces[0], up_hidden, preferred_element_type=jnp.float32)
    backward = jnp.einsum("bsd,hd->bsh", pieces[1], down_hidden, preferred_element_type=jnp.float32)
    before = before.reshape(-1, before.shape[-1])
    backward = backward.reshape(-1, backward.shape[-1])
    active = jax.nn.silu(before).astype(jnp.bfloat16)
    inner_grad = (backward * silu_slope(before)).astype(jnp.bfloat16)
    up_moved, down_moved = (
        lax.all_to_all(up_weight, "ctx", split_axis=2, concat_axis=1, tiled=True),
        lax.all_to_all(down_weight, "ctx", split_axis=2, concat_axis=1, tiled=True),
    )
    up_features = up_moved[0]
    down_features = down_moved[0]
    pieces = (
        lax.all_gather(active, "ctx", axis=1, tiled=True),
        lax.all_gather(inner_grad, "ctx", axis=1, tiled=True),
    )
    out_total = jnp.dot(pieces[0], down_features, preferred_element_type=jnp.float32)
    in_total = jnp.dot(pieces[1], up_features, preferred_element_type=jnp.float32)
    columns = down_features.shape[1]
    result = out_total.astype(jnp.bfloat16).reshape(groups, capacity, columns)
    input_grad = in_total.astype(jnp.bfloat16).reshape(groups, capacity, columns)
    back_rows, back_grad = (
        lax.all_to_all(result, "exp", split_axis=0, concat_axis=0, tiled=True),
        lax.all_to_all(input_grad, "exp", split_axis=0, concat_axis=0, tiled=True),
    )
    back_rows = back_rows.reshape(groups * capacity, columns)
    back_grad = back_grad.reshape(groups * capacity, columns)
    route_result = jnp.take(back_rows, target, axis=0).astype(jnp.float32)
    route_grad = jnp.take(back_grad, target, axis=0).astype(jnp.float32)
    combined = jnp.sum((route_result * share[:, None]).reshape(block_len, 2, columns), axis=1)
    collected = jnp.sum(route_grad.reshape(block_len, 2, columns), axis=1)
    combined_rows, collected_rows = (
        lax.all_to_all(combined, "ctx", split_axis=0, concat_axis=1, tiled=True),
        lax.all_to_all(collected, "ctx", split_axis=0, concat_axis=1, tiled=True),
    )
    layer_output = (hidden + combined_rows).astype(jnp.bfloat16)
    _, pull_expert = jax.vjp(lambda values: rms_gain(values, expert_gain), hidden)
    hidden_grad = cotangent.astype(jnp.float32) + pull_expert(collected_rows)[0]
    residual_grad = hidden_grad.astype(jnp.bfloat16)
    _, pull_mixer = jax.vjp(lambda values: rms_gain(values, mixer_gain), mixed)
    mixed_grad = pull_mixer(hidden_grad)[0].astype(jnp.bfloat16)
    grad_heads = lax.all_to_all(mixed_grad, "ctx", split_axis=1, concat_axis=0, tiled=True).reshape(
        length, local_heads, head_width
    )
    block_grad = jax.vmap(state_grad, in_axes=(1, 1, 0))(query_heads, grad_heads, decay_slopes)
    later = entering_2((block_fade, block_grad), "exp", chain, identity, True)[1]
    query_grad, key_grad, value_grad = jax.vmap(
        span_backward, in_axes=(1, 1, 1, 0, 0, 1, 0), out_axes=1
    )(query_heads, key_heads, value_heads, entering, decay_slopes, grad_heads, later)
    return (
        layer_output,
        residual_grad,
        query_grad.reshape(length, -1),
        key_grad.reshape(length, -1),
        value_grad.reshape(length, -1),
    )


def solution(mesh):
    in_specs = (
        P("exp", "ctx"),
        P("exp", "ctx"),
        P("exp", "ctx"),
        P("ctx"),
        P(("exp", "ctx"), None),
        P(),
        P(),
        P("exp", "ctx", None),
        P("exp", "ctx", None),
        P("exp", None),
        P("exp", None),
        P(("exp", "ctx"), None),
    )
    out_specs = (
        P(("exp", "ctx"), None),
        P(("exp", "ctx"), None),
        P("exp", "ctx"),
        P("exp", "ctx"),
        P("exp", "ctx"),
    )
    fast = mesh.shape["ctx"] == 8 and mesh.shape["exp"] == 4
    body = fast_device if fast else per_device
    return jax.shard_map(
        body, mesh=mesh, in_specs=in_specs, out_specs=out_specs, check_vma=False
    )
```

```python
import jax
import jax.numpy as jnp
from jax import lax
from jax.experimental import pallas as pl
from jax.experimental.pallas import tpu as pltpu
from jax.sharding import PartitionSpec as P

EPSILON = 1e-06
HIGHEST = lax.Precision.HIGHEST
BF16 = jnp.bfloat16
F32 = jnp.float32


def span_output(query_rows, key_rows, value_rows, entering, slope):
    length = query_rows.shape[0]
    places = jnp.arange(length).astype(jnp.float32)
    spacing = places[:, None] - places[None, :]
    fading = jnp.where(spacing >= 0.0, jnp.exp(-slope * jnp.maximum(spacing, 0.0)), 0.0)
    scores = jnp.dot(query_rows, key_rows.T, preferred_element_type=jnp.float32)
    weights = (scores * fading).astype(jnp.bfloat16)
    inner = jnp.dot(weights, value_rows, preferred_element_type=jnp.float32)
    carried = jnp.dot(query_rows.astype(jnp.float32), entering, precision=HIGHEST)
    return inner + carried * jnp.exp(-slope * (places + 1.0))[:, None]


def span_summary(key_rows, value_rows, slope):
    length = key_rows.shape[0]
    places = jnp.arange(length).astype(jnp.float32)
    faded = key_rows.astype(jnp.float32) * jnp.exp(-slope * (length - 1.0 - places))[:, None]
    return jnp.dot(faded.T, value_rows.astype(jnp.float32), precision=HIGHEST)


def span_pair(query_rows, key_rows, value_rows, entering, slope):
    return (
        span_output(query_rows, key_rows, value_rows, entering, slope),
        span_summary(key_rows, value_rows, slope),
    )


def state_grad(query_rows, grad_rows, slope):
    length = query_rows.shape[0]
    places = jnp.arange(length).astype(jnp.float32)
    faded = query_rows.astype(jnp.float32) * jnp.exp(-slope * (places + 1.0))[:, None]
    return jnp.dot(faded.T, grad_rows.astype(jnp.float32), precision=HIGHEST)


def span_backward(query_rows, key_rows, value_rows, entering, slope, grad_rows, grad_state):

    def local_pair(first, second, third):
        return span_pair(first, second, third, entering, slope)

    _, pullback = jax.vjp(local_pair, query_rows, key_rows, value_rows)
    return pullback((grad_rows.astype(jnp.float32), grad_state))


def silu_slope(before):
    sigma = jax.nn.sigmoid(before)
    return sigma * (1.0 + before * (1.0 - sigma))


def ring_order(size):
    if size == 8:
        return [0, 2, 4, 6, 7, 5, 3, 1]
    return list(range(size))


class Ring:
    def __init__(self):
        self.size = lax.axis_size("ctx")
        order = ring_order(self.size)
        self.right = [(order[i], order[(i + 1) % self.size]) for i in range(self.size)]
        self.left = [(b, a) for a, b in self.right]
        place = [order.index(i) for i in range(self.size)]
        self.order = jnp.array(order, jnp.int32)
        self.place = jnp.array(place, jnp.int32)[lax.axis_index("ctx")]

    def at(self, offset):
        return self.order[(self.place + offset) % self.size]

    def go_right(self, x):
        return lax.ppermute(x, "ctx", self.right)

    def go_left(self, x):
        return lax.ppermute(x, "ctx", self.left)


def swap(x, k):
    return lax.ppermute(x, "exp", [(i, i ^ k) for i in range(lax.axis_size("exp"))])


def ctx_sum(x):
    size = lax.axis_size("ctx")
    step = 1
    while step < size:
        x = x + lax.ppermute(x, "ctx", [(i, i ^ step) for i in range(size)])
        step *= 2
    return x


def ring_start(far, ring):
    low = far.astype(BF16)
    half = low.shape[0] // 2
    return ring.go_right(low[:half]), ring.go_left(low[half:])


def ring_sum(partial, start, ring):
    to_right, to_left = start
    blank = jnp.zeros_like(to_right)
    to_right = jnp.concatenate([to_right, blank], axis=0)
    to_left = jnp.concatenate([blank, to_left], axis=0)
    for offset in (3, 2, 1):
        to_right = ring.go_right((partial[offset] + to_right.astype(F32)).astype(BF16))
        to_left = ring.go_left((partial[-offset] + to_left.astype(F32)).astype(BF16))
    return partial[0] + to_right.astype(F32) + to_left.astype(F32)


def ring_block(size, offset):
    here = lax.axis_index("ctx")
    row, column = here // 2, here % 2
    place = row + column * (size - 1 - 2 * row)
    at = (place + offset + size) % size
    far = at // (size // 2)
    return 2 * at + far * (2 * size - 1 - 4 * at)


def columns(weight_ref, block, size):
    width = weight_ref.shape[1] // size
    return weight_ref[:, pl.ds(pl.multiple_of(block * width, width), width)]


WHOLE = pl.BlockSpec(memory_space=pltpu.VMEM)
ANYWHERE = pl.BlockSpec(memory_space=pl.ANY)
IN_HBM = pl.BlockSpec(memory_space=pltpu.HBM)
NT = (((1,), (1,)), ((), ()))


def cost(rows, hidden, width):
    return pl.CostEstimate(
        flops=2 * rows * hidden * width, bytes_accessed=2 * hidden * width, transcendentals=0
    )


def meet(*arrays):
    def kernel(*refs):
        pass

    return pl.pallas_call(
        kernel,
        in_specs=[ANYWHERE] * len(arrays),
        out_specs=[ANYWHERE] * len(arrays),
        out_shape=[jax.ShapeDtypeStruct(x.shape, x.dtype) for x in arrays],
        input_output_aliases={k: k for k in range(len(arrays))},
        name="meet",
    )(*arrays)


def backward_call(rows_all, weight, after=()):
    rows, features = rows_all.shape
    hidden = weight.shape[0]
    span, parts = rows // 4, 4
    part = features // parts

    def kernel(rows_ref, weight_ref, *refs):
        total, held, landed = refs[-3:]
        mine = lax.axis_index("exp")
        core, side = lax.rem(mine, 2), mine // 2

        def fetch(k):
            copies = []
            for j, (flip_side, flip_core) in enumerate(((0, 0), (1, 0), (0, 1), (1, 1))):
                block = 2 * (side + flip_side * (1 - 2 * side)) + core
                block = block + flip_core * (1 - 2 * core)
                copies.append(
                    pltpu.make_async_copy(
                        rows_ref.at[
                            pl.ds(pl.multiple_of(block * span, span), span),
                            pl.ds(k * part, part),
                        ],
                        held.at[k % 2, pl.ds(j * span, span), :],
                        landed.at[k % 2, j],
                    )
                )
                copies[-1].start()
            return copies

        coming = fetch(0)
        for k in range(parts):
            arrived = coming
            if k + 1 < parts:
                coming = fetch(k + 1)
            for copy in arrived:
                copy.wait()
            value = lax.dot_general(
                held[k % 2],
                weight_ref[:, pl.ds(k * part, part)],
                NT,
                preferred_element_type=F32,
            )
            total[...] = value if k == 0 else total[...] + value

    return pl.pallas_call(
        kernel,
        in_specs=[IN_HBM, WHOLE] + [ANYWHERE] * len(after),
        out_specs=WHOLE,
        out_shape=jax.ShapeDtypeStruct((rows, hidden), F32),
        scratch_shapes=[
            pltpu.VMEM((2, rows, part), BF16),
            pltpu.SemaphoreType.DMA((2, 4)),
        ],
        compiler_params=pltpu.CompilerParams(vmem_limit_bytes=10 * 2**20),
        cost_estimate=cost(rows, hidden, features),
        name="backward_rows",
    )(rows_all, weight, *after)


def before_call(found, ring, offsets, weight, gain, start=None, finish=None, after=()):
    count = len(offsets)
    pieces = [part for o in offsets for part in found[o]]
    span, width = pieces[0].shape
    rows, hidden, features, size = 4 * span, weight.shape[0], weight.shape[1], ring.size
    gain = gain.reshape(size, width)
    sums = [jax.ShapeDtypeStruct((rows, hidden), F32), jax.ShapeDtypeStruct((rows, 1), F32)]
    first, last = start is None, finish is not None

    def kernel(weight_ref, gain_ref, *refs):
        refs = list(refs)
        parts = [refs.pop(0) for _ in pieces]
        begin = [] if first else [refs.pop(0), refs.pop(0)]
        ending = [refs.pop(0), refs.pop(0)] if last else []
        refs = refs[len(after) :]
        outs = [refs.pop(0), refs.pop(0)]
        held, scaled, landed = refs[:3]
        total = refs[3] if last else outs[0]
        copies = []
        for k in range(count):
            for j in range(4):
                copies.append(
                    pltpu.make_async_copy(
                        parts[4 * k + j],
                        held.at[k, pl.ds(j * span, span), :],
                        landed.at[4 * k + j],
                    )
                )
                copies[-1].start()
        square = None if first else begin[1][...]
        for k in range(count):
            for copy in copies[4 * k : 4 * k + 4]:
                copy.wait()
            value = held[k].astype(F32)
            squares = jnp.sum(value * value, axis=-1, keepdims=True)
            square = squares if square is None else square + squares
            block = ring_block(size, offsets[k])
            scaled[...] = (value * gain_ref[pl.ds(block, 1), :]).astype(BF16)
            product = lax.dot_general(
                scaled[...], columns(weight_ref, block, size), NT, preferred_element_type=F32
            )
            if k == 0:
                total[...] = product if first else begin[0][...] + product
            else:
                total[...] += product
        if last:
            before = total[...] * lax.rsqrt(square / features + EPSILON)
            sigma = 1.0 / (1.0 + jnp.exp(-before))
            backward_ref, share_ref = ending
            share = share_ref[...]
            routed = share > 0.0
            outs[0][...] = jnp.where(routed, before * sigma, 0.0).astype(BF16)
            slope = sigma * (1.0 + before * (1.0 - sigma))
            inner = share * backward_ref[...] * slope
            outs[1][...] = jnp.where(routed, inner, 0.0).astype(BF16)
        else:
            outs[1][...] = square

    rest = list(start or ()) + list(finish or ())
    lows = [jax.ShapeDtypeStruct((rows, hidden), BF16)] * 2
    return pl.pallas_call(
        kernel,
        in_specs=[WHOLE, WHOLE]
        + [ANYWHERE] * len(pieces)
        + [WHOLE] * len(rest)
        + [ANYWHERE] * len(after),
        out_specs=[WHOLE, WHOLE],
        out_shape=lows if last else sums,
        scratch_shapes=[
            pltpu.VMEM((count, rows, width), BF16),
            pltpu.VMEM((rows, width), BF16),
            pltpu.SemaphoreType.DMA((4 * count,)),
        ]
        + ([pltpu.VMEM((rows, hidden), F32)] if last else []),
        compiler_params=pltpu.CompilerParams(vmem_limit_bytes=10 * 2**20),
        cost_estimate=cost(rows, hidden, count * width),
        name="before_rows",
    )(weight, gain, *pieces, *rest, *after)


def second_call(left, ring, offsets, weight, share=None, after=()):
    count = len(offsets)
    rows, hidden = left.shape
    half, size = rows // 2, ring.size
    width = weight.shape[1] // size

    def kernel(weight_ref, left_ref, *refs):
        keep_ref, give_ref = refs[-2:]
        for k in range(count):
            block = ring_block(size, offsets[k])
            value = jnp.dot(
                left_ref[...], columns(weight_ref, block, size), preferred_element_type=F32
            )
            if share is not None:
                value = value * refs[0][...]
            keep_ref[k] = value[:half].astype(BF16)
            give_ref[k] = value[half:].astype(BF16)

    extra = [] if share is None else [share]
    return pl.pallas_call(
        kernel,
        in_specs=[WHOLE] * (2 + len(extra)) + [ANYWHERE] * len(after),
        out_specs=[WHOLE, WHOLE],
        out_shape=[jax.ShapeDtypeStruct((count, half, width), BF16)] * 2,
        compiler_params=pltpu.CompilerParams(vmem_limit_bytes=8 * 2**20),
        cost_estimate=cost(rows, hidden, count * width),
        name="partial_rows",
    )(weight, left, *extra, *after)


def turn_call(residual, cotangent, ring, after):
    rows, features = residual.shape
    width = features // ring.size

    def kernel(residual_ref, cotangent_ref, *refs):
        out_ref = refs[-1]
        for k in range(ring.size):
            span = pl.ds(k * width, width)
            out_ref[k, pl.ds(0, rows), :] = residual_ref[:, span]
            out_ref[k, pl.ds(rows, rows), :] = cotangent_ref[:, span]

    return pl.pallas_call(
        kernel,
        in_specs=[WHOLE, WHOLE] + [ANYWHERE] * len(after),
        out_specs=WHOLE,
        out_shape=jax.ShapeDtypeStruct((ring.size, 2 * rows, width), BF16),
        name="turn",
    )(residual, cotangent, *after)


def fast_device(
    queries,
    key_vectors,
    value_vectors,
    decay_slopes,
    residual,
    mixer_gain,
    expert_gain,
    up_weight,
    down_weight,
    expert_ids,
    gate_code,
    cotangent,
):
    length, width = queries.shape
    features = residual.shape[1]
    local_heads = decay_slopes.shape[0]
    head_width = width // local_heads
    ring = Ring()
    here, mine = lax.axis_index("ctx"), lax.axis_index("exp")
    core = mine % 2

    cot_all = lax.all_gather(cotangent, ("exp", "ctx"), axis=0, tiled=True)

    codes = (expert_ids * 16 + gate_code).astype(F32)
    codes = jnp.concatenate([codes, swap(codes, 2)], axis=0)
    codes = jnp.concatenate([codes, swap(codes, 1)], axis=0).astype(jnp.int32)
    share = jnp.where(codes // 16 == mine, (1.0 + (codes % 16).astype(F32)) / 16.0, 0.0)
    share = jnp.sum(share, axis=-1, keepdims=True)

    query_heads = queries.reshape(length, local_heads, head_width)
    key_heads = key_vectors.reshape(length, local_heads, head_width)
    value_heads = value_vectors.reshape(length, local_heads, head_width)
    fade = jnp.exp(-decay_slopes * length)[:, None, None]
    summary = jax.vmap(span_summary, in_axes=(1, 1, 0))(key_heads, value_heads, decay_slopes)
    other = swap(summary, 1)
    pair = jnp.where(core == 0, fade * summary + other, fade * other + summary)
    both = turn_call(residual, cotangent, ring, (other, share))
    both = lax.all_to_all(both, "ctx", split_axis=0, concat_axis=0, tiled=True)
    both = both.reshape(ring.size, 2, -1, width)
    residual_part = both[:, 0].reshape(length, width)
    cot_part = both[:, 1].reshape(length, width)
    before_pair = lax.ppermute(pair, "exp", [(0, 2), (1, 3)])
    entering = jnp.where(core == 0, before_pair, fade * before_pair + other)
    mixed_heads = jax.vmap(span_output, in_axes=(1, 1, 1, 0, 0), out_axes=1)(
        query_heads, key_heads, value_heads, entering, decay_slopes
    )
    mixed_low = lax.optimization_barrier(mixed_heads.reshape(length, width).astype(BF16))
    mixed = mixed_low.astype(F32)
    mix_gain = lax.dynamic_slice(mixer_gain, (here * width,), (width,))
    exp_gain = lax.dynamic_slice(expert_gain, (here * width,), (width,))
    mixed_square = ctx_sum(jnp.sum(mixed * mixed, axis=-1)[None])[0][:, None]
    scale_1 = lax.rsqrt(mixed_square / features + EPSILON)
    hidden_low = (residual_part.astype(F32) + mixed * scale_1 * mix_gain).astype(BF16)
    hidden_low = lax.optimization_barrier(hidden_low)
    hidden = hidden_low.astype(F32)
    across = swap(hidden_low, 2)
    rights, lefts = [hidden_low], [hidden_low]
    for step in range(1, 4):
        right, left = meet(ring.go_right(rights[-1]), ring.go_left(lefts[-1]))
        rights.append(right)
        lefts.append(left)
    rights.append(ring.go_right(rights[-1]))
    cot = cot_part.astype(F32)
    early = jnp.stack(
        [
            jnp.sum(hidden * hidden, axis=-1),
            jnp.sum(mix_gain * mixed * cot, axis=-1),
            jnp.sum(mix_gain * mixed * hidden, axis=-1),
        ]
    )

    up_hidden = up_weight[0]
    found = {}
    for step in range(5):
        for offset, rows in ((-step, rights), (step, lefts)):
            if (step < 4 and (step > 0 or rows is rights)) or (step == 4 and rows is rights):
                own = rows[step]
                far = across if step == 0 else swap(own, 2)
                found[4 if step == 4 else offset] = (own, far, swap(own, 1), swap(far, 1))

    def before_part(offsets, sums=None, finish=None, after=()):
        return before_call(found, ring, offsets, up_hidden, expert_gain, sums, finish, after)

    sums = before_part((0,), after=(rights[3],))
    down_hidden = down_weight[0]
    backward = backward_call(cot_all, down_hidden, (rights[4], sums[1]))
    sums = before_part((-1, 1), sums, after=(backward,))
    sums = before_part((-2, 2), sums)
    sums = before_part((-3, 3), sums)
    active, inner_grad = before_part((4,), sums, (backward, share))

    in_parts, out_parts = {}, {}

    def second(left, offsets, weight, parts, scale, after):
        keep, give = second_call(left, ring, offsets, weight, scale, after)
        got = swap(give, 1)
        for i, offset in enumerate(offsets):
            parts[offset] = keep[i].astype(F32) + got[i].astype(F32)
        return give, got

    def second_in(offsets, *after):
        return second(inner_grad, offsets, up_hidden, in_parts, None, after)

    def second_out(offsets, *after):
        return second(active, offsets, down_hidden, out_parts, share, after)

    def cross(offsets):
        far = jnp.stack([in_parts[o][length:].astype(BF16) for o in offsets])
        far = swap(far, 2)
        for i, o in enumerate(offsets):
            in_parts[o] = in_parts[o][:length] + far[i].astype(F32)
        return far

    give, got_in_4 = second_in((4,))
    far_4 = cross((4,))
    give, got_out_4 = second_out((4,), give)
    out_start = ring_start(out_parts[4], ring)
    give, got_in_3 = second_in((3, -3), give)
    far_3 = cross((3, -3))
    give, got_out_3 = second_out((3, -3), give, got_in_4)
    give, got_in_2 = second_in((2, -2), give, got_out_4)
    far_2 = cross((2, -2))
    give, got_out_2 = second_out((2, -2), give, got_in_3)
    give, got_in_1 = second_in((1, -1), give, got_out_3, far_4)
    cross((1, -1))
    give, _ = second_out((1, -1), give, got_in_2, *out_start)
    give, _ = second_in((0,), give, far_3)
    cross((0,))
    second_out((0,), give, got_out_2, far_2)
    collected = ring_sum(in_parts, ring_start(in_parts[4], ring), ring)
    combined = ring_sum(out_parts, out_start, ring)
    combined = combined[:length] + swap(combined[length:].astype(BF16), 2).astype(F32)

    gained = exp_gain * collected
    late = jnp.stack(
        [jnp.sum(gained * hidden, axis=-1), jnp.sum(mix_gain * mixed * gained, axis=-1)]
    )
    hidden_square, along_cot, along_hidden, along_gained, along_mixed = ctx_sum(
        jnp.concatenate([early, late], axis=0)
    )[:, :, None]
    scale_2 = lax.rsqrt(hidden_square / features + EPSILON)
    pull_2 = scale_2 * scale_2 * scale_2 / features * along_gained
    hidden_grad = cot + scale_2 * gained - hidden * pull_2
    along = along_cot + scale_2 * along_mixed - pull_2 * along_hidden
    mixed_grad = scale_1 * (mix_gain * hidden_grad) - mixed * (
        scale_1 * scale_1 * scale_1 / features * along
    )
    grad_heads = lax.optimization_barrier(mixed_grad.astype(BF16))
    grad_heads = grad_heads.reshape(length, local_heads, head_width)
    ends = jnp.concatenate(
        [x.astype(BF16).reshape(ring.size, -1, width) for x in (hidden_grad, hidden + combined)],
        axis=1,
    )
    ends = lax.all_to_all(ends, "ctx", split_axis=0, concat_axis=0, tiled=True)
    ends = ends.transpose(1, 0, 2).reshape(2, -1, features)
    residual_grad, layer_output = ends[0], ends[1]

    block_grad = jax.vmap(state_grad, in_axes=(1, 1, 0))(query_heads, grad_heads, decay_slopes)
    other = swap(block_grad, 1)
    pair = jnp.where(core == 0, block_grad + fade * other, other + fade * block_grad)
    after_pair = lax.ppermute(pair, "exp", [(2, 0), (3, 1)])
    later = jnp.where(core == 0, other + fade * after_pair, after_pair)
    query_grad, key_grad, value_grad = jax.vmap(
        span_backward, in_axes=(1, 1, 1, 0, 0, 1, 0), out_axes=1
    )(query_heads, key_heads, value_heads, entering, decay_slopes, grad_heads, later)
    return (
        layer_output,
        residual_grad,
        query_grad.reshape(length, -1),
        key_grad.reshape(length, -1),
        value_grad.reshape(length, -1),
    )


def entering_2(x, axis, combine, identity, reverse):
    count, position = (lax.axis_size(axis), lax.axis_index(axis))
    everything = jax.tree.map(lambda part: lax.all_gather(part, axis), x)
    start = jax.tree.map(
        lambda part, zero: jnp.broadcast_to(jnp.asarray(zero, part.dtype), part.shape), x, identity
    )

    def lap(k, before):
        at = count - 1 - k if reverse else k
        reached = at > position if reverse else at < position
        new = combine(before, jax.tree.map(lambda part: part[at], everything))
        return jax.tree.map(lambda a, b: jnp.where(reached, a, b), new, before)

    return lax.fori_loop(0, count, lap, start)


def rms_gain(values, gain):
    return values * lax.rsqrt(jnp.mean(values * values, axis=-1, keepdims=True) + EPSILON) * gain


def chain(earlier, later):
    return (earlier[0] * later[0], later[0][:, None, None] * earlier[1] + later[1])


def per_device(
    queries,
    key_vectors,
    value_vectors,
    decay_slopes,
    residual,
    mixer_gain,
    expert_gain,
    up_weight,
    down_weight,
    expert_ids,
    gate_code,
    cotangent,
):
    length = queries.shape[0]
    local_heads = decay_slopes.shape[0]
    head_width = queries.shape[1] // local_heads
    query_heads = queries.reshape(length, local_heads, head_width)
    key_heads = key_vectors.reshape(length, local_heads, head_width)
    value_heads = value_vectors.reshape(length, local_heads, head_width)
    block_fade = jnp.exp(-decay_slopes * length)
    summary = jax.vmap(span_summary, in_axes=(1, 1, 0))(key_heads, value_heads, decay_slopes)
    identity = (jnp.ones_like(block_fade), jnp.zeros_like(summary))
    entering = entering_2((block_fade, summary), "exp", chain, identity, False)[1]
    mixed_heads = jax.vmap(span_output, in_axes=(1, 1, 1, 0, 0), out_axes=1)(
        query_heads, key_heads, value_heads, entering, decay_slopes
    )
    mixed_heads = mixed_heads.astype(jnp.bfloat16).reshape(length, -1)
    mixed_low = lax.all_to_all(mixed_heads, "ctx", split_axis=0, concat_axis=1, tiled=True)
    mixed = mixed_low.astype(jnp.float32)
    hidden_low = (residual.astype(jnp.float32) + rms_gain(mixed, mixer_gain)).astype(jnp.bfloat16)
    hidden = lax.optimization_barrier(hidden_low).astype(jnp.float32)
    normed = rms_gain(hidden, expert_gain).astype(jnp.bfloat16)
    groups = lax.axis_size("exp")
    block_len = expert_ids.shape[0]
    capacity = min(block_len, max(2, 17 * block_len // (8 * groups)))
    share = ((1.0 + gate_code.astype(jnp.float32)) / 16.0).reshape(-1)
    flat = expert_ids.reshape(-1)
    marks = (flat[:, None] == jnp.arange(groups, dtype=jnp.int32)[None, :]).astype(jnp.int32)
    slots = jnp.sum((jnp.cumsum(marks, axis=0) - marks) * marks, axis=1)
    target = flat * capacity + slots
    matching = target[None, :] == jnp.arange(groups * capacity, dtype=jnp.int32)[:, None]
    filled = jnp.any(matching, axis=1)
    source_route = jnp.sum(
        jnp.where(matching, jnp.arange(2 * block_len, dtype=jnp.int32)[None, :], 0), axis=1
    )
    source_token = source_route // 2
    slot_share = jnp.take(share, source_route)
    up_hidden = up_weight[0]
    down_hidden = down_weight[0]
    block_normed, block_cot = (
        lax.all_gather(normed, "ctx", axis=0, tiled=True),
        lax.all_gather(cotangent, "ctx", axis=0, tiled=True),
    )
    taken = jnp.take(block_normed, source_token, axis=0)
    rows = jnp.where(filled[:, None], taken, jnp.zeros_like(taken))
    weighted = jnp.take(block_cot, source_token, axis=0).astype(jnp.float32) * slot_share[:, None]
    grads = jnp.where(filled[:, None], weighted, 0.0).astype(jnp.bfloat16)
    send_rows = rows.reshape(groups, capacity, -1)
    send_grad = grads.reshape(groups, capacity, -1)
    pieces = (
        lax.all_to_all(send_rows, "exp", split_axis=0, concat_axis=0, tiled=True),
        lax.all_to_all(send_grad, "exp", split_axis=0, concat_axis=0, tiled=True),
    )
    before = jnp.einsum("bsd,hd->bsh", pieces[0], up_hidden, preferred_element_type=jnp.float32)
    backward = jnp.einsum("bsd,hd->bsh", pieces[1], down_hidden, preferred_element_type=jnp.float32)
    before = before.reshape(-1, before.shape[-1])
    backward = backward.reshape(-1, backward.shape[-1])
    active = jax.nn.silu(before).astype(jnp.bfloat16)
    inner_grad = (backward * silu_slope(before)).astype(jnp.bfloat16)
    up_moved, down_moved = (
        lax.all_to_all(up_weight, "ctx", split_axis=2, concat_axis=1, tiled=True),
        lax.all_to_all(down_weight, "ctx", split_axis=2, concat_axis=1, tiled=True),
    )
    up_features = up_moved[0]
    down_features = down_moved[0]
    pieces = (
        lax.all_gather(active, "ctx", axis=1, tiled=True),
        lax.all_gather(inner_grad, "ctx", axis=1, tiled=True),
    )
    out_total = jnp.dot(pieces[0], down_features, preferred_element_type=jnp.float32)
    in_total = jnp.dot(pieces[1], up_features, preferred_element_type=jnp.float32)
    columns = down_features.shape[1]
    result = out_total.astype(jnp.bfloat16).reshape(groups, capacity, columns)
    input_grad = in_total.astype(jnp.bfloat16).reshape(groups, capacity, columns)
    back_rows, back_grad = (
        lax.all_to_all(result, "exp", split_axis=0, concat_axis=0, tiled=True),
        lax.all_to_all(input_grad, "exp", split_axis=0, concat_axis=0, tiled=True),
    )
    back_rows = back_rows.reshape(groups * capacity, columns)
    back_grad = back_grad.reshape(groups * capacity, columns)
    route_result = jnp.take(back_rows, target, axis=0).astype(jnp.float32)
    route_grad = jnp.take(back_grad, target, axis=0).astype(jnp.float32)
    combined = jnp.sum((route_result * share[:, None]).reshape(block_len, 2, columns), axis=1)
    collected = jnp.sum(route_grad.reshape(block_len, 2, columns), axis=1)
    combined_rows, collected_rows = (
        lax.all_to_all(combined, "ctx", split_axis=0, concat_axis=1, tiled=True),
        lax.all_to_all(collected, "ctx", split_axis=0, concat_axis=1, tiled=True),
    )
    layer_output = (hidden + combined_rows).astype(jnp.bfloat16)
    _, pull_expert = jax.vjp(lambda values: rms_gain(values, expert_gain), hidden)
    hidden_grad = cotangent.astype(jnp.float32) + pull_expert(collected_rows)[0]
    residual_grad = hidden_grad.astype(jnp.bfloat16)
    _, pull_mixer = jax.vjp(lambda values: rms_gain(values, mixer_gain), mixed)
    mixed_grad = pull_mixer(hidden_grad)[0].astype(jnp.bfloat16)
    grad_heads = lax.all_to_all(mixed_grad, "ctx", split_axis=1, concat_axis=0, tiled=True).reshape(
        length, local_heads, head_width
    )
    block_grad = jax.vmap(state_grad, in_axes=(1, 1, 0))(query_heads, grad_heads, decay_slopes)
    later = entering_2((block_fade, block_grad), "exp", chain, identity, True)[1]
    query_grad, key_grad, value_grad = jax.vmap(
        span_backward, in_axes=(1, 1, 1, 0, 0, 1, 0), out_axes=1
    )(query_heads, key_heads, value_heads, entering, decay_slopes, grad_heads, later)
    return (
        layer_output,
        residual_grad,
        query_grad.reshape(length, -1),
        key_grad.reshape(length, -1),
        value_grad.reshape(length, -1),
    )


def solution(mesh):
    in_specs = (
        P("exp", "ctx"),
        P("exp", "ctx"),
        P("exp", "ctx"),
        P("ctx"),
        P(("exp", "ctx"), None),
        P(),
        P(),
        P("exp", "ctx", None),
        P("exp", "ctx", None),
        P("exp", None),
        P("exp", None),
        P(("exp", "ctx"), None),
    )
    out_specs = (
        P(("exp", "ctx"), None),
        P(("exp", "ctx"), None),
        P("exp", "ctx"),
        P("exp", "ctx"),
        P("exp", "ctx"),
    )
    fast = mesh.shape["ctx"] == 8 and mesh.shape["exp"] == 4
    body = fast_device if fast else per_device
    return jax.shard_map(
        body, mesh=mesh, in_specs=in_specs, out_specs=out_specs, check_vma=False
    )
```
